32 devices in a mesh: fsdp: 4 (over y, core), seq: 8 (over z, x).
Axes of the slice: x: 2, y: 2, z: 4, core: 2. Of those that a mesh axis runs over, the one named last changes fastest.
Arguments:
- hidden_in: bfloat16 [8, 1024, 2048], P('fsdp', 'seq'), may hold values from -6 to 6
- cotangent: bfloat16 [8, 1024, 2048], P('fsdp', 'seq'), may hold values from -6 to 6
- lengths: int32 [8], P('fsdp'), may hold values from 256 to 1024, as said below
- norm_gain: float32 [2048], replicated, may hold values from 0.5 to 1.5
- w_in: bfloat16 [2048, 8192], P('fsdp'), may hold values from -0.125 to 0.125
- conv_w: float32 [4, 4096], P(None, 'seq'), may hold values from -3 to 3
- conv_b: float32 [4096], P('seq'), may hold values from -1 to 1
- x_proj: bfloat16 [160, 4096], P(None, 'seq'), may hold values from -0.09375 to 0.09375
- dt_proj_w: bfloat16 [128, 4096], P(None, 'seq'), may hold values from -0.5 to 0.5
- dt_bias: float32 [4096], P('seq'), may hold values from -4.5 to -1
- a_log: float32 [16, 4096], P(None, 'seq'), may hold values from 0 to 2.77
- d_skip: float32 [4096], P('seq'), may hold values from 0.5 to 1.5
- w_out: bfloat16 [2048, 4096], P('fsdp'), may hold values from -0.1875 to 0.1875
Outputs:
- block_out: bfloat16 [8, 1024, 2048], P('fsdp', 'seq')
- grad_in: bfloat16 [8, 1024, 2048], P('fsdp', 'seq')
- grad_gain: float32 [2048], replicated
- grad_w_in: float32 [2048, 8192], P(('fsdp', 'seq'))
- grad_conv_w: float32 [4, 4096], P(None, 'seq')
- grad_conv_b: float32 [4096], P('seq')
- grad_x_proj: float32 [160, 4096], P(None, 'seq')
- grad_dt_proj: float32 [128, 4096], P(None, 'seq')
- grad_dt_bias: float32 [4096], P('seq')
- grad_a_log: float32 [16, 4096], P(None, 'seq')
- grad_d_skip: float32 [4096], P('seq')
- grad_w_out: float32 [2048, 4096], P(('fsdp', 'seq'))
The draws below stay inside these ranges and needn't reach their ends.
Inputs may be any that keep to these rules, and one draw needn't show every extreme that they name: `lengths`: sequence g * 2 + m is micro-batch m of index g of fsdp; in every index one of its 2 sequences has all 1024 positions, and some sequence has exactly 256.
All inputs are finite; a program needn't handle non-finite values.
Results may differ from the reference program's by a relative error of at most 0.012.
Values may be sent and summed in bfloat16 or wider, within the bound.
No kernel may reach another device: no remote copies, remote signals or barrier semaphores. Data moves between devices by JAX's collectives and lax.ppermute only.
A program may use at most 304 MiB of HBM per device.

```python
import jax
import jax.numpy as jnp
from jax import lax

D = 2048
DI = 4096
NS = 16
DTR = 128
CONV = 4
MICRO = 2
LEN = 1024
SEQS = 8
PROJ_ROWS = 160


def draw_lengths(key, part):
    key = jax.random.fold_in(key, 11)
    key_random, key_full, key_short = jax.random.split(key, 3)
    groups = SEQS // MICRO
    drawn_lengths = jax.random.randint(key_random, (groups, MICRO), LEN // 4, LEN + 1)
    full_choice = jax.random.randint(key_full, (groups, 1), 0, MICRO)
    members = jnp.arange(MICRO)[None, :]
    drawn_lengths = jnp.where(members == full_choice, LEN, drawn_lengths)
    short_group = jax.random.randint(key_short, (), 0, groups)
    short_member = (full_choice[short_group, 0] + 1) % MICRO
    group_rows = jnp.arange(groups)[:, None]
    drawn_lengths = jnp.where((group_rows == short_group) & (members == short_member) & (short_member != full_choice[short_group, 0]), LEN // 4, drawn_lengths)
    return drawn_lengths.reshape(SEQS).astype(jnp.int32)


def with_spikes(drawn, key, source, target, blocks, factor):
    owner, partner = [(jnp.arange(drawn.shape[axis_at]) // (drawn.shape[axis_at] // blocks)).reshape([-1 if axis == axis_at else 1 for axis in range(drawn.ndim)]) for axis_at in (source, target)]
    chosen = jax.random.permutation(key, blocks)[partner]
    strong = (owner == chosen) | (owner == (partner + blocks // 2) % blocks)
    return jnp.where(strong, factor * drawn, drawn)


def block_levels(rng, shape, cuts, smallest, largest):
    def one(dim, blocks):
        steps = jax.random.uniform(jax.random.fold_in(jax.random.fold_in(rng, 6), dim), (blocks,), jnp.float32, smallest / len(cuts), largest / len(cuts))
        return jnp.repeat(jnp.exp(steps), shape[dim] // blocks).reshape((-1,) + (1,) * (len(shape) - dim - 1))

    loudness = one(*cuts[0])
    for cut in cuts[1:]:
        loudness = loudness * one(*cut)
    return loudness


def scatter_about(rng, extent, deviation, reach, shards=(), kind=jnp.bfloat16):
    factor_of = block_levels(rng, extent, shards, -0.22, 0.18) if shards else 1.0
    array = jax.random.normal(rng, extent, jnp.float32) * deviation * factor_of
    return jnp.minimum(jnp.maximum(array, -reach), reach).astype(kind)


def heavy_noise(key, shape, width, reach, shards, heavy, kind=jnp.bfloat16):
    values = width * jax.random.normal(key, shape, jnp.float32)
    if shards:
        values = values * block_levels(key, shape, shards, -0.22, 0.18)
    return jnp.clip(with_spikes(values, jax.random.fold_in(key, 3), *heavy), -reach, reach).astype(kind)


def setup_inputs(seed: int = 0) -> dict:
    seeds = jax.random.split(jax.random.key(seed), 14)
    hidden_in = heavy_noise(seeds[0], (SEQS, LEN, D), 1.0, 6.0, ((0, 4), (1, 8)), (1, 2, 8, 2.0))
    cotangent = heavy_noise(seeds[1], (SEQS, LEN, D), 1.0, 6.0, ((0, 4), (1, 8)), (1, 2, 8, 2.0))
    lengths = draw_lengths(jax.random.fold_in(seeds[13], 71), 0)
    norm_gain = jnp.clip(jax.random.uniform(seeds[3], (D,), jnp.float32, 0.5, 1.5), 0.5, 1.5)
    w_in = scatter_about(seeds[4], (D, 2 * DI), D ** -0.5, 0.125, ((0, 4),))
    conv_w = scatter_about(seeds[5], (CONV, DI), CONV ** -0.5, 3.0, ((1, 8),), jnp.float32)
    conv_b = jnp.clip(jax.random.uniform(seeds[6], (DI,), jnp.float32, -1.0, 1.0) * block_levels(seeds[6], (DI,), ((0, 8),), -0.4, 0.0), -1.0, 1.0)
    x_proj = scatter_about(seeds[7], (PROJ_ROWS, DI), DI ** -0.5, 0.09375, ((1, 8),))
    dt_proj_w = scatter_about(seeds[8], (DTR, DI), DTR ** -0.5, 0.5, ((1, 8),))
    dt_bias = jnp.clip(-4.5 + 3.5 * jax.random.uniform(seeds[9], (DI,), jnp.float32) ** block_levels(seeds[9], (DI,), ((0, 8),), -0.2, 0.2), -4.5, -1.0)
    a_log = jnp.clip(2.77 * jax.random.uniform(seeds[10], (NS, DI), jnp.float32) ** block_levels(seeds[10], (NS, DI), ((1, 8),), -0.2, 0.2), 0.0, 2.77)
    d_skip = jnp.clip(0.5 + 1.0 * jax.random.uniform(seeds[11], (DI,), jnp.float32) ** block_levels(seeds[11], (DI,), ((0, 8),), -0.2, 0.2), 0.5, 1.5)
    w_out = scatter_about(seeds[12], (D, DI), (DI // 4) ** -0.5, 0.1875, ((0, 4),))
    return {"hidden_in": hidden_in, "cotangent": cotangent, "lengths": lengths, "norm_gain": norm_gain, "w_in": w_in, "conv_w": conv_w, "conv_b": conv_b, "x_proj": x_proj, "dt_proj_w": dt_proj_w, "dt_bias": dt_bias, "a_log": a_log, "d_skip": d_skip, "w_out": w_out}


EPS = 1e-05
HIGH = lax.Precision.HIGHEST

@jax.custom_vjp
def low(v):
    return lax.optimization_barrier(v.astype(jnp.bfloat16)).astype(jnp.float32)

@jax.custom_vjp
def low_back(v):
    return v

def low_keep(v):
    return (low(v), None)

def low_pass(kept, grad):
    return (grad,)

def back_keep(v):
    return (v, None)

def back_low(kept, grad):
    return (low(grad),)
low.defvjp(low_keep, low_pass)
low_back.defvjp(back_keep, back_low)

def scan_stretch(carried, pieces, rates):

    def one_step(hidden, slot_values):
        step_sizes, step_input, step_entry, step_readout = slot_values
        hidden = jnp.exp(step_sizes[None, :] * rates) * hidden + step_entry[:, None] * (step_sizes * step_input)[None, :]
        return (hidden, lax.optimization_barrier(jnp.sum(step_readout[:, None] * hidden, axis=0)))
    return lax.scan(one_step, carried, pieces)

def selective_scan(step_sizes, u_values, entry_columns, readout_columns, rates):
    block_rows = min(256, LEN)
    block_count = LEN // block_rows
    pieces = tuple((series.reshape((block_count, block_rows) + series.shape[1:]) for series in (step_sizes, u_values, entry_columns, readout_columns)))

    def outer_step(carried, slot_values):
        return jax.checkpoint(scan_stretch)(carried, slot_values, rates)
    initial = jnp.zeros((NS, DI), jnp.float32)
    _, outputs = lax.scan(outer_step, initial, pieces)
    return outputs.reshape(LEN, DI)

def block_forward(seq_in, valid_rows, norm_gain, w_in, conv_w, conv_b, x_proj, dt_proj_w, dt_bias, a_log, d_skip, w_out):
    inverse = lax.rsqrt(lax.optimization_barrier(jnp.mean(seq_in * seq_in, axis=-1, keepdims=True)) + EPS)
    normed = low(seq_in * inverse * norm_gain)
    projected = low_back(jnp.dot(normed, w_in, precision=HIGH))
    x_part = low(projected[:, :DI])
    z_part = projected[:, DI:]
    padded = jnp.concatenate([jnp.zeros((CONV - 1, DI), jnp.float32), x_part], axis=0)
    pre_conv = conv_b + sum((conv_w[offset] * padded[offset:offset + LEN] for offset in range(CONV)))
    u_act = low(jax.nn.silu(pre_conv))
    select = low_back(jnp.dot(x_proj, u_act.T, precision=HIGH))
    size_low = low(select[:DTR])
    entry_rows = select[DTR:DTR + NS]
    readout_rows = select[DTR + NS:]
    size_pre = low_back(jnp.dot(size_low.T, dt_proj_w, precision=HIGH) + dt_bias)
    step_sizes = jax.nn.softplus(size_pre)
    rates = -jnp.exp(a_log)
    scanned = selective_scan(step_sizes, u_act, entry_rows.T, readout_rows.T, rates) + d_skip * u_act
    y_sent = low_back(low(scanned))
    gated = low(y_sent * jax.nn.silu(z_part))
    branch = low_back(jnp.dot(gated, w_out.T, precision=HIGH))
    return seq_in + valid_rows[:, None] * branch

def add_pair(running, latest):
    return running + latest

def reference(hidden_in, cotangent, lengths, norm_gain, w_in, conv_w, conv_b, x_proj, dt_proj_w, dt_bias, a_log, d_skip, w_out):
    weights = (norm_gain, w_in.astype(jnp.float32), conv_w, conv_b, x_proj.astype(jnp.float32), dt_proj_w.astype(jnp.float32), dt_bias, a_log, d_skip, w_out.astype(jnp.float32))
    positions = jnp.arange(LEN, dtype=jnp.int32)

    def per_sequence(totals, slot_values):
        seq_in, seq_cot, seq_length = slot_values
        valid_rows = (positions < seq_length).astype(jnp.float32)

        def forward(seq_values, weight_list):
            return block_forward(seq_values, valid_rows, *weight_list)
        result, pullback = jax.vjp(forward, seq_in.astype(jnp.float32), weights)
        grad_seq, grad_weights = pullback(seq_cot.astype(jnp.float32))
        totals = jax.tree.map(add_pair, totals, grad_weights)
        return (totals, (result.astype(jnp.bfloat16), grad_seq.astype(jnp.bfloat16)))
    initial = jax.tree.map(jnp.zeros_like, weights)
    totals, (outputs, grads) = lax.scan(per_sequence, initial, (hidden_in, cotangent, lengths))
    return (outputs, grads, totals[0], totals[1], totals[2], totals[3], totals[4], totals[5], totals[6], totals[7], totals[8], totals[9])
```

```python
from functools import partial

import jax
import jax.numpy as jnp
from jax import lax
from jax.experimental import pallas as pl
from jax.experimental.pallas import tpu as pltpu
from jax.sharding import PartitionSpec as P

EPS = 1e-05
LOG2E = 1.4426950408889634
NT = (((1,), (1,)), ((), ()))
TN = (((0,), (0,)), ((), ()))
ROWS = 128
SUB = 16


def softplus(x):
    e = jnp.exp(-jnp.abs(x))
    return jnp.maximum(x, 0.0) + jnp.log1p(e)


def block_diagonal(columns, states):
    wide = SUB * states
    lane = lax.broadcasted_iota(jnp.int32, (states, wide), 1)
    row = lax.broadcasted_iota(jnp.int32, (states, wide), 0)
    tile = (lax.rem(lane, states) == row).astype(jnp.bfloat16)
    spread = lax.dot_general(columns.astype(jnp.bfloat16), tile, TN, preferred_element_type=jnp.float32)
    block = lax.broadcasted_iota(jnp.int32, (ROWS, wide), 1) // states
    step = lax.rem(lax.broadcasted_iota(jnp.int32, (ROWS, wide), 0), SUB)
    return jnp.where(block == step, spread, 0.0).astype(jnp.bfloat16)


def scan_forward_kernel(
    low_rank, states, lanes,
    sel_ref, u_ref, dtp_ref, bias_ref, alog_ref, skip_ref,
    y_ref, h_ref, delta_ref, sig_ref,
    state, pre, weighted, diag, decay,
):
    chan = u_ref.shape[1]

    @pl.when(pl.program_id(0) == 0)
    def _():
        state[...] = jnp.zeros_like(state)
        decay[...] = -jnp.exp(alog_ref[...]) * LOG2E

    low = sel_ref[:low_rank, :].astype(jnp.bfloat16)
    pre[...] = lax.dot_general(low, dtp_ref[...], TN, preferred_element_type=jnp.float32)
    entry = sel_ref[low_rank : low_rank + states, :]
    diag[...] = block_diagonal(sel_ref[low_rank + states :, :], states)

    def piece(sub, _):
        base = pl.multiple_of(sub * SUB, SUB)
        rows = pl.ds(base, SUB)
        size = pre[rows, :] + bias_ref[...]
        delta = softplus(size)
        delta_ref[rows, :] = delta
        sig_ref[rows, :] = jnp.exp(size - delta).astype(jnp.bfloat16)
        u_float = u_ref[rows, :].astype(jnp.float32)
        weighted[rows, :] = delta * u_float
        cols = pltpu.roll(entry, lax.rem(ROWS - base, ROWS), 1)
        for start in range(0, chan, lanes):
            at = pl.ds(start, lanes)
            rate = decay[:, at]
            hidden = state[:, at]
            for step in range(SUB):
                row = pl.ds(base + step, 1)
                grow = jnp.exp2(delta_ref[row, at] * rate)
                hidden = grow * hidden + cols[:, step : step + 1] * weighted[row, at]
                h_ref[pl.ds(pl.multiple_of((base + step) * states, states), states), at] = hidden.astype(jnp.bfloat16)
            state[:, at] = hidden
            held = h_ref[pl.ds(pl.multiple_of(base * states, SUB * states), SUB * states), at]
            out = jnp.dot(diag[rows, :], held, preferred_element_type=jnp.float32)
            y_ref[rows, at] = (out + skip_ref[:, at] * u_float[:, start : start + lanes]).astype(jnp.bfloat16)
        return 0

    lax.fori_loop(0, ROWS // SUB, piece, 0)


def scan_forward(select, u_act, dt_proj, dt_bias, a_log, d_skip):
    length, chan = u_act.shape
    states = a_log.shape[0]
    low_rank = dt_proj.shape[0]
    lanes = min(256, chan)
    whole = lambda shape: pl.BlockSpec(shape, lambda i: (0, 0))
    by_rows = pl.BlockSpec((ROWS, chan), lambda i: (i, 0))
    return pl.pallas_call(
        partial(scan_forward_kernel, low_rank, states, lanes),
        grid=(length // ROWS,),
        in_specs=[
            pl.BlockSpec((select.shape[0], ROWS), lambda i: (0, i)),
            by_rows,
            whole((low_rank, chan)),
            whole((1, chan)),
            whole((states, chan)),
            whole((1, chan)),
        ],
        out_specs=[by_rows, pl.BlockSpec((ROWS * states, chan), lambda i: (i, 0)), by_rows, by_rows],
        out_shape=[
            jax.ShapeDtypeStruct((length, chan), jnp.bfloat16),
            jax.ShapeDtypeStruct((length * states, chan), jnp.bfloat16),
            jax.ShapeDtypeStruct((length, chan), jnp.float32),
            jax.ShapeDtypeStruct((length, chan), jnp.bfloat16),
        ],
        scratch_shapes=[
            pltpu.VMEM((states, chan), jnp.float32),
            pltpu.VMEM((ROWS, chan), jnp.float32),
            pltpu.VMEM((ROWS, chan), jnp.float32),
            pltpu.VMEM((ROWS, SUB * states), jnp.bfloat16),
            pltpu.VMEM((states, chan), jnp.float32),
        ],
        compiler_params=pltpu.CompilerParams(vmem_limit_bytes=40 * 2**20),
        cost_estimate=pl.CostEstimate(
            flops=12 * length * states * chan,
            bytes_accessed=length * chan * (2 * states + 10),
            transcendentals=length * states * chan,
        ),
        name="scan_forward",
    )(select, u_act, dt_proj, dt_bias.reshape(1, chan), a_log, d_skip.reshape(1, chan))


def scan_backward_kernel(
    low_rank, states, lanes,
    sel_ref, h_ref, before_ref, delta_ref, sig_ref, u_ref, dy_ref, alog_ref, skip_ref,
    pre_ref, upart_ref, ent_ref, rdo_ref, dec_ref, bias_ref, skipg_ref,
    carry, dyf, weighted, diag, decay, rates16, gbuf, abuf, dbuf,
):
    chan = u_ref.shape[1]
    wide = SUB * states
    step_id = pl.program_id(0)
    last = pl.num_programs(0) - 1

    @pl.when(step_id == 0)
    def _():
        carry[...] = jnp.zeros_like(carry)
        rates = -jnp.exp(alog_ref[...])
        decay[...] = rates * LOG2E
        rates16[...] = rates.astype(jnp.bfloat16)
        dec_ref[...] = jnp.zeros_like(dec_ref)
        bias_ref[...] = jnp.zeros_like(bias_ref)
        skipg_ref[...] = jnp.zeros_like(skipg_ref)

    readout = sel_ref[low_rank + states :, :]
    diag[...] = block_diagonal(sel_ref[low_rank : low_rank + states, :], states)
    block = lax.broadcasted_iota(jnp.int32, (SUB, wide), 1) // states
    inside = block == lax.broadcasted_iota(jnp.int32, (SUB, wide), 0)
    ones = jnp.where(inside, 1.0, 0.0).astype(jnp.bfloat16)
    member = lax.rem(lax.broadcasted_iota(jnp.int32, (states, wide), 1), states)
    gather = jnp.where(member == lax.broadcasted_iota(jnp.int32, (states, wide), 0), 1.0, 0.0).astype(jnp.bfloat16)

    def piece(index, _):
        sub = ROWS // SUB - 1 - index
        base = pl.multiple_of(sub * SUB, SUB)
        rows = pl.ds(base, SUB)
        hrows = pl.ds(pl.multiple_of(base * states, wide), wide)
        u_float = u_ref[rows, :].astype(jnp.float32)
        delta = delta_ref[rows, :]
        dy_float = dy_ref[rows, :].astype(jnp.float32)
        dyf[...] = dy_float
        weighted[...] = (delta * u_float).astype(jnp.bfloat16)
        cols = pltpu.roll(readout, lax.rem(ROWS - base, ROWS), 1)
        first = lax.max(base * states - states, 0)
        ent = jnp.zeros((SUB, wide), jnp.float32)
        rdo = jnp.zeros((SUB, wide), jnp.float32)
        for start in range(0, chan, lanes):
            at = pl.ds(start, lanes)
            rate = decay[:, at]
            rate16 = rates16[:, at]
            passed = carry[:, at]
            inner = h_ref[pl.ds(pl.multiple_of(first, states), states), at]
            outer = jnp.where(step_id == last, jnp.zeros_like(inner), before_ref[:, at])
            earliest = jnp.where(sub == 0, outer, inner)
            for step in reversed(range(SUB)):
                row = pl.ds(base + step, 1)
                size = jnp.broadcast_to(delta_ref[row, at], (states, lanes))
                grow = jnp.exp2(size * rate)
                grad = cols[:, step : step + 1] * dyf[pl.ds(step, 1), at] + passed
                passed = grow * grad
                if step:
                    earlier = h_ref[pl.ds(pl.multiple_of((base + step - 1) * states, states), states), at]
                else:
                    earlier = earliest
                logg = passed.astype(jnp.bfloat16) * earlier
                here = pl.ds(step * states, states)
                gbuf[here, at] = grad.astype(jnp.bfloat16)
                abuf[here, at] = logg * rate16
                dbuf[here, at] = logg * size.astype(jnp.bfloat16)
            carry[:, at] = passed
            shared = jnp.dot(diag[rows, :], gbuf[:, at], preferred_element_type=jnp.float32)
            size_a = jnp.dot(ones, abuf[:, at], preferred_element_type=jnp.float32)
            dec_ref[:, at] += jnp.dot(gather, dbuf[:, at], preferred_element_type=jnp.float32)
            rdo += lax.dot_general(dy_ref[rows, at], h_ref[hrows, at], NT, preferred_element_type=jnp.float32)
            ent += lax.dot_general(weighted[:, at], gbuf[:, at], NT, preferred_element_type=jnp.float32)
            u_here = u_float[:, start : start + lanes]
            dy_here = dy_float[:, start : start + lanes]
            pre16 = ((size_a + shared * u_here) * sig_ref[rows, at].astype(jnp.float32)).astype(jnp.bfloat16)
            pre_ref[rows, at] = pre16
            bias_ref[:, at] += jnp.sum(pre16.astype(jnp.float32), axis=0, keepdims=True)
            skipg_ref[:, at] += jnp.sum(dy_here * u_here, axis=0, keepdims=True)
            upart_ref[rows, at] = shared * delta[:, start : start + lanes] + skip_ref[:, at] * dy_here
        ent_ref[pl.ds(sub, 1), :] = jnp.sum(jnp.where(inside, ent, 0.0), axis=0, keepdims=True)
        rdo_ref[pl.ds(sub, 1), :] = jnp.sum(jnp.where(inside, rdo, 0.0), axis=0, keepdims=True)
        return 0

    lax.fori_loop(0, ROWS // SUB, piece, 0)

    @pl.when(step_id == last)
    def _():
        dec_ref[...] = dec_ref[...] * -jnp.exp(alog_ref[...])


def scan_backward(select, hidden, delta, sig, u_act, y_grad, a_log, d_skip, low_rank):
    length, chan = u_act.shape
    states = a_log.shape[0]
    lanes = min(256, chan)
    wide = SUB * states
    count = length // ROWS
    whole = lambda shape: pl.BlockSpec(shape, lambda i: (0, 0))
    by_rows = pl.BlockSpec((ROWS, chan), lambda i: (count - 1 - i, 0))
    flat = pl.BlockSpec((ROWS // SUB, wide), lambda i: (count - 1 - i, 0))
    outs = pl.pallas_call(
        partial(scan_backward_kernel, low_rank, states, lanes),
        grid=(count,),
        in_specs=[
            pl.BlockSpec((select.shape[0], ROWS), lambda i: (0, count - 1 - i)),
            pl.BlockSpec((ROWS * states, chan), lambda i: (count - 1 - i, 0)),
            pl.BlockSpec((states, chan), lambda i: (jnp.maximum((count - 1 - i) * ROWS - 1, 0), 0)),
            by_rows,
            by_rows,
            by_rows,
            by_rows,
            whole((states, chan)),
            whole((1, chan)),
        ],
        out_specs=[by_rows, by_rows, flat, flat, whole((states, chan)), whole((1, chan)), whole((1, chan))],
        out_shape=[
            jax.ShapeDtypeStruct((length, chan), jnp.bfloat16),
            jax.ShapeDtypeStruct((length, chan), jnp.float32),
            jax.ShapeDtypeStruct((length // SUB, wide), jnp.float32),
            jax.ShapeDtypeStruct((length // SUB, wide), jnp.float32),
            jax.ShapeDtypeStruct((states, chan), jnp.float32),
            jax.ShapeDtypeStruct((1, chan), jnp.float32),
            jax.ShapeDtypeStruct((1, chan), jnp.float32),
        ],
        scratch_shapes=[
            pltpu.VMEM((states, chan), jnp.float32),
            pltpu.VMEM((SUB, chan), jnp.float32),
            pltpu.VMEM((SUB, chan), jnp.bfloat16),
            pltpu.VMEM((ROWS, wide), jnp.bfloat16),
            pltpu.VMEM((states, chan), jnp.float32),
            pltpu.VMEM((states, chan), jnp.bfloat16),
            pltpu.VMEM((wide, chan), jnp.bfloat16),
            pltpu.VMEM((wide, chan), jnp.bfloat16),
            pltpu.VMEM((wide, chan), jnp.bfloat16),
        ],
        compiler_params=pltpu.CompilerParams(vmem_limit_bytes=40 * 2**20),
        cost_estimate=pl.CostEstimate(
            flops=30 * length * states * chan,
            bytes_accessed=length * chan * (2 * states + 16),
            transcendentals=length * states * chan,
        ),
        name="scan_backward",
    )(select, hidden, hidden, delta, sig, u_act, y_grad, a_log, d_skip.reshape(1, chan))
    pre_grad, u_part, entry, readout, dec, bias, skip = outs
    return pre_grad, u_part, entry.reshape(length, states), readout.reshape(length, states), dec, bias[0], skip[0]


def silu_slope(values):
    sigmoid_value = jax.nn.sigmoid(values)
    return sigmoid_value * (1.0 + values * (1.0 - sigmoid_value))


def swap(values, axis, size, bit):
    return lax.ppermute(values, axis, [(index, index ^ bit) for index in range(size)])


def orders(size):
    bits = [1 << place for place in range(size.bit_length() - 1)]
    return [bits[turn:] + bits[:turn] for turn in range(len(bits))] or [[]]


def cut(values, count, axis):
    width = values.shape[axis] // count
    return [lax.slice_in_dim(values, at * width, (at + 1) * width, axis=axis) for at in range(count)]


def sum_over_group(values, size, group, axis):
    ways = orders(group)
    done = []
    for part, way in zip(cut(values, len(ways), axis), ways):
        for bit in way:
            part = part + swap(part, "seq", size, bit)
        done.append(part)
    return jnp.concatenate(done, axis=axis)


def gather_tokens(blocks, size, group, place, half):
    rows, width = blocks.shape[1:]
    mine = lax.dynamic_index_in_dim(blocks, half, 0, keepdims=False)
    other = swap(lax.dynamic_index_in_dim(blocks, 1 - half, 0, keepdims=False), "seq", size, group)
    ways = orders(group)
    parts = len(ways)
    buffer = jnp.zeros((size, rows, width), blocks.dtype)
    for source, side in ((mine, half), (other, 1 - half)):
        for at, (part, way) in enumerate(zip(cut(source, parts, 1), ways)):
            held = [(0, part)]
            for bit in way:
                sent = swap(jnp.stack([piece for _, piece in held]), "seq", size, bit)
                held = held + [(offset ^ bit, sent[index]) for index, (offset, _) in enumerate(held)]
            for offset, piece in held:
                where = side * group + (place ^ offset)
                buffer = lax.dynamic_update_slice(buffer, piece[None], (where, 0, at * (width // parts)))
    return buffer


def scatter_tokens(total, size, group, place, half):
    rows, width = total.shape[1:]
    ways = orders(group)
    done = []
    for part, way in zip(cut(total.reshape(2, group, rows, width), len(ways), 3), ways):
        held = [(offset, None) for offset in range(group)]
        part = {offset: lax.dynamic_index_in_dim(part, place ^ offset, 1, keepdims=False) for offset in range(group)}
        for bit in way:
            keep = [offset for offset in part if not offset & bit]
            sent = swap(jnp.stack([part[offset ^ bit] for offset in keep]).astype(jnp.bfloat16), "seq", size, bit)
            part = {offset: part[offset] + sent[index].astype(jnp.float32) for index, offset in enumerate(keep)}
        done.append(part[0])
    both = jnp.concatenate(done, axis=2)
    mine = lax.dynamic_index_in_dim(both, half, 0, keepdims=False)
    other = lax.dynamic_index_in_dim(both, 1 - half, 0, keepdims=False).astype(jnp.bfloat16)
    other = swap(other, "seq", size, group).astype(jnp.float32)
    first = jnp.where(half == 0, mine, other)
    second = jnp.where(half == 0, other, mine)
    return jnp.stack([first, second])


def own_columns(weight, start, cols, place, group):
    return jnp.concatenate(
        [lax.dynamic_slice_in_dim(weight, start + (place + turn * group) * cols, cols, 1) for turn in range(2)], axis=1
    )


def both_blocks(values, size, group, half):
    other = swap(values, "seq", size, group)
    return jnp.concatenate([jnp.where(half == 0, values, other), jnp.where(half == 0, other, values)], axis=-1)


def rows_to_owner(partial_sum, size, group):
    reduced = lax.psum_scatter(partial_sum, "fsdp", scatter_dimension=0, tiled=True)
    rows, cols = reduced.shape
    pieces = lax.all_to_all(reduced.reshape(size, rows // size, cols), "seq", split_axis=0, concat_axis=0, tiled=True)
    pieces = pieces.reshape(2, group, rows // size, 2, cols // 2).astype(jnp.float32)
    summed = pieces[0] + pieces[1]
    return jnp.transpose(summed, (1, 2, 0, 3)).reshape(rows // size, group * cols)


def shards(
    hidden_in,
    cotangent,
    lengths,
    norm_gain,
    w_in,
    conv_w,
    conv_b,
    x_proj,
    dt_proj_w,
    dt_bias,
    a_log,
    d_skip,
    w_out,
):
    size = lax.axis_size("seq")
    group = size // 2
    index = lax.axis_index("seq")
    half, place = index // group, index % group
    rows_dev, width = hidden_in.shape[1:]
    length = size * rows_dev
    cols = conv_b.shape[0]
    inner = w_out.shape[1]
    states, low_rank = a_log.shape[0], dt_proj_w.shape[0]
    taps = conv_w.shape[0]
    bf16, f32 = jnp.bfloat16, jnp.float32

    w_x = lax.all_gather(own_columns(w_in, 0, cols, place, group), "fsdp", axis=0, tiled=True)
    w_z = lax.all_gather(own_columns(w_in, inner, cols, place, group), "fsdp", axis=0, tiled=True)
    w_o = lax.all_gather(own_columns(w_out, 0, cols, place, group), "fsdp", axis=0, tiled=True)

    flat = hidden_in.astype(f32)
    inverse = lax.rsqrt(jnp.mean(flat * flat, axis=-1, keepdims=True) + EPS)
    scaled = flat * inverse
    tokens = gather_tokens((scaled * norm_gain).astype(bf16), size, group, place, half).reshape(length, width)

    small = jnp.concatenate([conv_w, conv_b[None], dt_bias[None], a_log, d_skip[None]], axis=0)
    small = both_blocks(small, size, group, half)
    conv_taps, conv_bias, step_bias = small[:taps], small[taps], small[taps + 1]
    log_rates, skip = small[taps + 2 : taps + 2 + states], small[taps + 2 + states]
    proj = both_blocks(jnp.concatenate([x_proj, dt_proj_w], axis=0), size, group, half)
    sel_proj, size_proj = proj[: x_proj.shape[0]], proj[x_proj.shape[0] :]

    positions = lax.iota(jnp.int32, length)
    valid = (positions < lax.dynamic_index_in_dim(lengths, half, 0, keepdims=False)).astype(f32)[:, None]
    cot = gather_tokens(cotangent, size, group, place, half).reshape(length, width)

    x_part = jnp.dot(tokens, w_x, preferred_element_type=f32).astype(bf16)
    x_float = jnp.pad(x_part.astype(f32), ((taps - 1, 0), (0, 0)))
    pre_conv = conv_bias + sum(conv_taps[at] * x_float[at : at + length] for at in range(taps))
    u_act = jax.nn.silu(pre_conv).astype(bf16)
    select = lax.dot_general(sel_proj, u_act, NT, preferred_element_type=f32)
    select = sum_over_group(select, size, group, 1)
    z_part = jnp.dot(tokens, w_z, preferred_element_type=f32)
    branch_grad = (cot.astype(f32) * valid).astype(bf16)
    gated_grad = jnp.dot(branch_grad, w_o, preferred_element_type=f32)
    z_gate = jax.nn.silu(z_part)
    y_grad = (gated_grad * z_gate).astype(bf16)

    y_sent, held, delta, sig = scan_forward(select, u_act, size_proj, step_bias, log_rates, skip)
    y_float = y_sent.astype(f32)
    gated = (y_float * z_gate).astype(bf16)
    z_grad = (gated_grad * y_float * silu_slope(z_part)).astype(bf16)

    branch = lax.dot_general(gated, w_o, NT, preferred_element_type=f32)
    branch = scatter_tokens(branch.reshape(size, rows_dev, width), size, group, place, half)
    own = index * rows_dev + lax.iota(jnp.int32, rows_dev)
    own_valid = (own[None] < lengths[:, None]).astype(f32)[..., None]
    block_out = (flat + own_valid * branch).astype(bf16)

    out_part = lax.dot_general(branch_grad, gated, TN, preferred_element_type=f32)
    grad_w_out = rows_to_owner(out_part, size, group)
    z_term = lax.dot_general(tokens, z_grad, TN, preferred_element_type=f32)
    grad_w_z = rows_to_owner(z_term, size, group)

    pre_grad, u_part, entry, readout, log_grad, bias_grad, skip_grad = scan_backward(
        select, held, delta, sig, u_act, y_grad, log_rates, skip, low_rank
    )
    low_grad = lax.dot_general(size_proj, pre_grad, NT, preferred_element_type=f32)
    select_part = jnp.concatenate([low_grad, entry.T, readout.T], axis=0)
    select_grad = sum_over_group(select_part, size, group, 1).astype(bf16)
    proj_grad = jnp.dot(select[:low_rank].astype(bf16), pre_grad, preferred_element_type=f32)
    sel_grad = jnp.dot(select_grad, u_act, preferred_element_type=f32)

    u_grad = u_part + lax.dot_general(select_grad, sel_proj, TN, preferred_element_type=f32)
    conv_grad = u_grad * silu_slope(pre_conv)
    convb_grad = jnp.sum(conv_grad, axis=0)
    convw_grad = jnp.stack([jnp.sum(conv_grad * x_float[at : at + length], axis=0) for at in range(taps)])
    late = jnp.pad(conv_grad, ((0, taps - 1), (0, 0)))
    x_grad = sum(conv_taps[at] * late[taps - 1 - at : taps - 1 - at + length] for at in range(taps)).astype(bf16)

    normed_grad = lax.dot_general(x_grad, w_x, NT, preferred_element_type=f32)
    normed_grad = normed_grad + lax.dot_general(z_grad, w_z, NT, preferred_element_type=f32)
    normed_grad = scatter_tokens(normed_grad.reshape(size, rows_dev, width), size, group, place, half)
    scaled_grad = normed_grad * norm_gain
    grad_in = cotangent.astype(f32) + inverse * (
        scaled_grad - scaled * jnp.mean(scaled_grad * scaled, axis=-1, keepdims=True)
    )

    x_term = lax.dot_general(tokens, x_grad, TN, preferred_element_type=f32)
    grad_w_x = rows_to_owner(x_term, size, group)
    gain_part = jnp.sum(w_x.astype(f32) * x_term, axis=1) + jnp.sum(w_z.astype(f32) * z_term, axis=1)
    grad_gain = lax.psum(gain_part, ("fsdp", "seq")) / norm_gain

    stacked = jnp.concatenate(
        [convw_grad, convb_grad[None], sel_grad, proj_grad, bias_grad[None], log_grad, skip_grad[None]], axis=0
    )
    mine = lax.dynamic_slice_in_dim(stacked, half * cols, cols, 1)
    other = swap(lax.dynamic_slice_in_dim(stacked, (1 - half) * cols, cols, 1), "seq", size, group)
    stacked = lax.psum(mine + other, "fsdp")
    pieces = []
    at = 0
    for count in (taps, 1, x_proj.shape[0], low_rank, 1, states, 1):
        pieces.append(stacked[at : at + count])
        at += count
    convw, convb, xproj, dtproj, dtbias, alog, dskip = pieces
    return (
        block_out,
        grad_in.astype(bf16),
        grad_gain,
        jnp.concatenate([grad_w_x, grad_w_z], axis=1),
        convw,
        convb[0],
        xproj,
        dtproj,
        dtbias[0],
        alog,
        dskip[0],
        grad_w_out,
    )


def solution(mesh):
    return jax.shard_map(
        shards,
        mesh=mesh,
        in_specs=(
            P("fsdp", "seq", None),
            P("fsdp", "seq", None),
            P("fsdp"),
            P(),
            P("fsdp", None),
            P(None, "seq"),
            P("seq"),
            P(None, "seq"),
            P(None, "seq"),
            P("seq"),
            P(None, "seq"),
            P("seq"),
            P("fsdp", None),
        ),
        out_specs=(
            P("fsdp", "seq", None),
            P("fsdp", "seq", None),
            P(),
            P(("fsdp", "seq"), None),
            P(None, "seq"),
            P("seq"),
            P(None, "seq"),
            P(None, "seq"),
            P("seq"),
            P(None, "seq"),
            P("seq"),
            P(("fsdp", "seq"), None),
        ),
        check_vma=False,
    )
```

```python
from functools import partial

import jax
import jax.numpy as jnp
from jax import lax
from jax.experimental import pallas as pl
from jax.experimental.pallas import tpu as pltpu
from jax.sharding import Mesh
from jax.sharding import PartitionSpec as P

EPS = 1e-05
LOG2E = 1.4426950408889634
NT = (((1,), (1,)), ((), ()))
TN = (((0,), (0,)), ((), ()))
ROWS = 128
LANES = 256
SUB = 16


def gate(values, *earlier):
    count = len(values)
    anywhere = pl.BlockSpec(memory_space=pl.ANY)
    return pl.pallas_call(
        lambda *refs: None,
        in_specs=[anywhere] * (count + len(earlier)),
        out_specs=[anywhere] * count,
        out_shape=[jax.ShapeDtypeStruct(value.shape, value.dtype) for value in values],
        input_output_aliases={at: at for at in range(count)},
        name="gate",
    )(*values, *earlier)


def softplus(x):
    e = jnp.exp(-jnp.abs(x))
    return jnp.maximum(x, 0.0) + jnp.log1p(e)


def block_diagonal(columns, states):
    wide = SUB * states
    lane = lax.broadcasted_iota(jnp.int32, (states, wide), 1)
    row = lax.broadcasted_iota(jnp.int32, (states, wide), 0)
    tile = (lax.rem(lane, states) == row).astype(jnp.bfloat16)
    spread = lax.dot_general(columns.astype(jnp.bfloat16), tile, TN, preferred_element_type=jnp.float32)
    block = lax.broadcasted_iota(jnp.int32, (ROWS, wide), 1) // states
    step = lax.rem(lax.broadcasted_iota(jnp.int32, (ROWS, wide), 0), SUB)
    return jnp.where(block == step, spread, 0.0).astype(jnp.bfloat16)


def scan_forward_kernel(
    low_rank, states, lanes,
    order_ref, sel_ref, u_ref, dtp_ref, bias_ref, alog_ref, skip_ref, start_ref,
    *refs,
):
    y_ref, h_ref, delta_ref, sig_ref, end_ref, state, pre, weighted, diag, decay = refs[-10:]
    chan = u_ref.shape[1]

    @pl.when(pl.program_id(0) == 0)
    def _():
        state[...] = start_ref[...]
        decay[...] = -jnp.exp(alog_ref[...]) * LOG2E

    low = sel_ref[:low_rank, :].astype(jnp.bfloat16)
    pre[...] = lax.dot_general(low, dtp_ref[...], TN, preferred_element_type=jnp.float32)
    entry = sel_ref[low_rank : low_rank + states, :]
    diag[...] = block_diagonal(sel_ref[low_rank + states :, :], states)

    def piece(sub, _):
        base = pl.multiple_of(sub * SUB, SUB)
        rows = pl.ds(base, SUB)
        size = pre[rows, :] + bias_ref[...]
        delta = softplus(size)
        delta_ref[rows, :] = delta
        sig_ref[rows, :] = jnp.exp(size - delta).astype(jnp.bfloat16)
        u_float = u_ref[rows, :].astype(jnp.float32)
        weighted[rows, :] = delta * u_float
        cols = pltpu.roll(entry, lax.rem(ROWS - base, ROWS), 1)
        for start in range(0, chan, lanes):
            at = pl.ds(start, lanes)
            rate = decay[:, at]
            hidden = state[:, at]
            for step in range(SUB):
                row = pl.ds(base + step, 1)
                grow = jnp.exp2(delta_ref[row, at] * rate)
                hidden = grow * hidden + cols[:, step : step + 1] * weighted[row, at]
                h_ref[pl.ds(pl.multiple_of((base + step) * states, states), states), at] = hidden.astype(jnp.bfloat16)
            state[:, at] = hidden
            held = h_ref[pl.ds(pl.multiple_of(base * states, SUB * states), SUB * states), at]
            out = jnp.dot(diag[rows, :], held, preferred_element_type=jnp.float32)
            y_ref[rows, at] = (out + skip_ref[:, at] * u_float[:, start : start + lanes]).astype(jnp.bfloat16)
        return 0

    lax.fori_loop(0, ROWS // SUB, piece, 0)
    end_ref[...] = state[...]


def scan_forward(order, first, count, select, u_act, dt_proj, dt_bias, a_log, d_skip, start, held=(), needs=()):
    length, chan = u_act.shape
    states = a_log.shape[0]
    low_rank = dt_proj.shape[0]
    lanes = min(LANES, chan)
    whole = lambda shape: pl.BlockSpec(shape, lambda i, order: (0, 0))
    by_rows = pl.BlockSpec((ROWS, chan), lambda i, order: (order[first + i], 0))
    in_time = pl.BlockSpec((ROWS, chan), lambda i, order: (i, 0))
    spec = pltpu.PrefetchScalarGridSpec(
        num_scalar_prefetch=1,
        grid=(count,),
        in_specs=[
            pl.BlockSpec((select.shape[0], ROWS), lambda i, order: (0, first + i)),
            by_rows,
            whole((low_rank, chan)),
            whole((1, chan)),
            whole((states, chan)),
            whole((1, chan)),
            whole((states, chan)),
        ]
        + [pl.BlockSpec(memory_space=pl.ANY)] * (len(held) + len(needs)),
        out_specs=[
            by_rows,
            pl.BlockSpec((ROWS * states, chan), lambda i, order: (i, 0)),
            in_time,
            in_time,
            whole((states, chan)),
        ],
        scratch_shapes=[
            pltpu.VMEM((states, chan), jnp.float32),
            pltpu.VMEM((ROWS, chan), jnp.float32),
            pltpu.VMEM((ROWS, chan), jnp.float32),
            pltpu.VMEM((ROWS, SUB * states), jnp.bfloat16),
            pltpu.VMEM((states, chan), jnp.float32),
        ],
    )
    rows = count * ROWS
    return pl.pallas_call(
        partial(scan_forward_kernel, low_rank, states, lanes),
        grid_spec=spec,
        out_shape=[
            jax.ShapeDtypeStruct((length, chan), jnp.bfloat16),
            jax.ShapeDtypeStruct((rows * states, chan), jnp.bfloat16),
            jax.ShapeDtypeStruct((rows, chan), jnp.float32),
            jax.ShapeDtypeStruct((rows, chan), jnp.bfloat16),
            jax.ShapeDtypeStruct((states, chan), jnp.float32),
        ],
        input_output_aliases={8 + at: at for at in range(len(held))},
        compiler_params=pltpu.CompilerParams(vmem_limit_bytes=40 * 2**20),
        cost_estimate=pl.CostEstimate(
            flops=12 * rows * states * chan,
            bytes_accessed=140 * rows * chan,
            transcendentals=rows * states * chan,
        ),
        name="scan_forward",
    )(order, select, u_act, dt_proj, dt_bias.reshape(1, chan), a_log, d_skip.reshape(1, chan), start, *held, *needs)


def scan_backward_kernel(
    low_rank, states, lanes,
    order_ref, sel_ref, h_ref, before_ref, start_ref, delta_ref, sig_ref, u_ref, dy_ref, dtp_ref, alog_ref, skip_ref,
    passed_ref, dec_in, bias_in, skip_in, proj_in,
    *refs,
):
    upart_ref, part_ref, dec_ref, bias_ref, skipg_ref, proj_ref, left_ref = refs[-19:-12]
    carry, dyf, weighted, diag, decay, rates16, gbuf, abuf, dbuf, ents, rdos, pre_ref = refs[-12:]
    chan = u_ref.shape[1]
    wide = SUB * states
    step_id = pl.program_id(0)
    last = pl.num_programs(0) - 1

    @pl.when(step_id == 0)
    def _():
        carry[...] = passed_ref[...]
        rates = -jnp.exp(alog_ref[...])
        decay[...] = rates * LOG2E
        rates16[...] = rates.astype(jnp.bfloat16)
        dec_ref[...] = dec_in[...]
        bias_ref[...] = bias_in[...]
        skipg_ref[...] = skip_in[...]
        proj_ref[...] = proj_in[...]

    readout = sel_ref[low_rank + states :, :]
    diag[...] = block_diagonal(sel_ref[low_rank : low_rank + states, :], states)
    block = lax.broadcasted_iota(jnp.int32, (SUB, wide), 1) // states
    inside = block == lax.broadcasted_iota(jnp.int32, (SUB, wide), 0)
    ones = jnp.where(inside, 1.0, 0.0).astype(jnp.bfloat16)
    member = lax.rem(lax.broadcasted_iota(jnp.int32, (states, wide), 1), states)
    gather = jnp.where(member == lax.broadcasted_iota(jnp.int32, (states, wide), 0), 1.0, 0.0).astype(jnp.bfloat16)

    def piece(index, _):
        sub = ROWS // SUB - 1 - index
        base = pl.multiple_of(sub * SUB, SUB)
        rows = pl.ds(base, SUB)
        hrows = pl.ds(pl.multiple_of(base * states, wide), wide)
        u_float = u_ref[rows, :].astype(jnp.float32)
        delta = delta_ref[rows, :]
        dy_float = dy_ref[rows, :].astype(jnp.float32)
        dyf[...] = dy_float
        weighted[...] = (delta * u_float).astype(jnp.bfloat16)
        cols = pltpu.roll(readout, lax.rem(ROWS - base, ROWS), 1)
        first = lax.max(base * states - states, 0)
        ent = jnp.zeros((SUB, wide), jnp.float32)
        rdo = jnp.zeros((SUB, wide), jnp.float32)
        for start in range(0, chan, lanes):
            at = pl.ds(start, lanes)
            rate = decay[:, at]
            rate16 = rates16[:, at]
            passed = carry[:, at]
            inner = h_ref[pl.ds(pl.multiple_of(first, states), states), at]
            outer = jnp.where(step_id == last, start_ref[:, at].astype(jnp.bfloat16), before_ref[:, at])
            earliest = jnp.where(sub == 0, outer, inner)
            for step in reversed(range(SUB)):
                row = pl.ds(base + step, 1)
                size = jnp.broadcast_to(delta_ref[row, at], (states, lanes))
                grow = jnp.exp2(size * rate)
                grad = cols[:, step : step + 1] * dyf[pl.ds(step, 1), at] + passed
                passed = grow * grad
                if step:
                    earlier = h_ref[pl.ds(pl.multiple_of((base + step - 1) * states, states), states), at]
                else:
                    earlier = earliest
                logg = passed.astype(jnp.bfloat16) * earlier
                here = pl.ds(step * states, states)
                gbuf[here, at] = grad.astype(jnp.bfloat16)
                abuf[here, at] = logg * rate16
                dbuf[here, at] = logg * size.astype(jnp.bfloat16)
            carry[:, at] = passed
            shared = jnp.dot(diag[rows, :], gbuf[:, at], preferred_element_type=jnp.float32)
            size_a = jnp.dot(ones, abuf[:, at], preferred_element_type=jnp.float32)
            dec_ref[:, at] += jnp.dot(gather, dbuf[:, at], preferred_element_type=jnp.float32)
            rdo += lax.dot_general(dy_ref[rows, at], h_ref[hrows, at], NT, preferred_element_type=jnp.float32)
            ent += lax.dot_general(weighted[:, at], gbuf[:, at], NT, preferred_element_type=jnp.float32)
            u_here = u_float[:, start : start + lanes]
            dy_here = dy_float[:, start : start + lanes]
            pre16 = ((size_a + shared * u_here) * sig_ref[rows, at].astype(jnp.float32)).astype(jnp.bfloat16)
            pre_ref[rows, at] = pre16
            bias_ref[:, at] += jnp.sum(pre16.astype(jnp.float32), axis=0, keepdims=True)
            skipg_ref[:, at] += jnp.sum(dy_here * u_here, axis=0, keepdims=True)
            upart_ref[rows, at] = shared * delta[:, start : start + lanes] + skip_ref[:, at] * dy_here
        ents[rows, :] = jnp.where(inside, ent, 0.0)
        rdos[rows, :] = jnp.where(inside, rdo, 0.0)
        return 0

    lax.fori_loop(0, ROWS // SUB, piece, 0)
    part_ref[:low_rank, :] = lax.dot_general(dtp_ref[...], pre_ref[...], NT, preferred_element_type=jnp.float32)
    low = sel_ref[:low_rank, :].astype(jnp.bfloat16)
    proj_ref[...] += jnp.dot(low, pre_ref[...], preferred_element_type=jnp.float32)
    whole = gather.astype(jnp.float32)
    for at, rows in ((low_rank, ents), (low_rank + states, rdos)):
        part_ref[at : at + states, :] = lax.dot_general(
            whole, rows[...], NT, precision=lax.Precision.HIGHEST, preferred_element_type=jnp.float32
        )
    left_ref[...] = carry[...]


def scan_backward(
    order, first, count, select, hidden, start, delta, sig, u_act, y_grad, dt_proj, a_log, d_skip, passed, sums, held=(), needs=()
):
    length, chan = u_act.shape
    states = a_log.shape[0]
    low_rank = dt_proj.shape[0]
    lanes = min(LANES, chan)
    wide = SUB * states
    rows = count * ROWS
    here = lambda i: count - 1 - i
    whole = lambda shape: pl.BlockSpec(shape, lambda i, order: (0, 0))
    by_rows = pl.BlockSpec((ROWS, chan), lambda i, order: (order[first + here(i)], 0))
    in_time = pl.BlockSpec((ROWS, chan), lambda i, order: (here(i), 0))
    by_cols = pl.BlockSpec((select.shape[0], ROWS), lambda i, order: (0, first + here(i)))
    before = pl.BlockSpec((states, chan), lambda i, order: (lax.max(here(i) - 1, 0) * ROWS + ROWS - 1, 0))
    spec = pltpu.PrefetchScalarGridSpec(
        num_scalar_prefetch=1,
        grid=(count,),
        in_specs=[
            by_cols,
            pl.BlockSpec((ROWS * states, chan), lambda i, order: (here(i), 0)),
            before,
            whole((states, chan)),
            in_time,
            in_time,
            by_rows,
            by_rows,
            whole((low_rank, chan)),
            whole((states, chan)),
            whole((1, chan)),
            whole((states, chan)),
            whole((states, chan)),
            whole((1, chan)),
            whole((1, chan)),
            whole((low_rank, chan)),
        ]
        + [pl.BlockSpec(memory_space=pl.ANY)] * (len(held) + len(needs)),
        out_specs=[
            pl.BlockSpec((ROWS, chan), lambda i, order: (first + here(i), 0)),
            by_cols,
            whole((states, chan)),
            whole((1, chan)),
            whole((1, chan)),
            whole((low_rank, chan)),
            whole((states, chan)),
        ],
        scratch_shapes=[
            pltpu.VMEM((states, chan), jnp.float32),
            pltpu.VMEM((SUB, chan), jnp.float32),
            pltpu.VMEM((SUB, chan), jnp.bfloat16),
            pltpu.VMEM((ROWS, wide), jnp.bfloat16),
            pltpu.VMEM((states, chan), jnp.float32),
            pltpu.VMEM((states, chan), jnp.bfloat16),
            pltpu.VMEM((wide, chan), jnp.bfloat16),
            pltpu.VMEM((wide, chan), jnp.bfloat16),
            pltpu.VMEM((wide, chan), jnp.bfloat16),
            pltpu.VMEM((ROWS, wide), jnp.float32),
            pltpu.VMEM((ROWS, wide), jnp.float32),
            pltpu.VMEM((ROWS, chan), jnp.bfloat16),
        ],
    )
    return pl.pallas_call(
        partial(scan_backward_kernel, low_rank, states, lanes),
        grid_spec=spec,
        out_shape=[
            jax.ShapeDtypeStruct((length, chan), jnp.float32),
            jax.ShapeDtypeStruct(select.shape, jnp.float32),
            jax.ShapeDtypeStruct((states, chan), jnp.float32),
            jax.ShapeDtypeStruct((1, chan), jnp.float32),
            jax.ShapeDtypeStruct((1, chan), jnp.float32),
            jax.ShapeDtypeStruct((low_rank, chan), jnp.float32),
            jax.ShapeDtypeStruct((states, chan), jnp.float32),
        ],
        input_output_aliases={17 + at: at for at in range(len(held))},
        compiler_params=pltpu.CompilerParams(vmem_limit_bytes=40 * 2**20),
        cost_estimate=pl.CostEstimate(
            flops=30 * rows * states * chan,
            bytes_accessed=220 * rows * chan,
            transcendentals=rows * states * chan,
        ),
        name="scan_backward",
    )(
        order, select, hidden, hidden, start, delta, sig, u_act, y_grad, dt_proj, a_log, d_skip.reshape(1, chan),
        passed, *sums, *held, *needs,
    )


def taps_of(window, rows, count):
    return [window[8 - (count - 1) + tap : 8 - (count - 1) + tap + rows, :] for tap in range(count)]


def conv_forward_kernel(lanes, order_ref, x_ref, w_ref, b_ref, proj_ref, *refs):
    u_ref, part_ref, tail = refs[-3:]
    rows, chan = x_ref.shape
    taps = w_ref.shape[0]

    @pl.when(pl.program_id(0) == 0)
    def _():
        tail[...] = jnp.zeros_like(tail)

    total = jnp.zeros(part_ref.shape, jnp.float32)
    for start in range(0, chan, lanes):
        at = pl.ds(start, lanes)
        values = x_ref[:, at].astype(jnp.float32)
        window = jnp.concatenate([tail[:, at], values], axis=0)
        tail[:, at] = values[rows - 8 :, :]
        pre = b_ref[:, at] + sum(w_ref[tap : tap + 1, at] * part for tap, part in enumerate(taps_of(window, rows, taps)))
        act = (pre / (1.0 + jnp.exp(-pre))).astype(jnp.bfloat16)
        u_ref[:, at] = act
        total = total + lax.dot_general(proj_ref[:, at], act, NT, preferred_element_type=jnp.float32)
    part_ref[...] = total


def conv_forward(order, x_part, conv_w, conv_b, sel_proj, needs=()):
    length, chan = x_part.shape
    wide = sel_proj.shape[0]
    whole = lambda shape: pl.BlockSpec(shape, lambda i, order: (0, 0))
    by_rows = pl.BlockSpec((ROWS, chan), lambda i, order: (order[i], 0))
    spec = pltpu.PrefetchScalarGridSpec(
        num_scalar_prefetch=1,
        grid=(length // ROWS,),
        in_specs=[by_rows, whole(conv_w.shape), whole((1, chan)), whole((wide, chan))]
        + [pl.BlockSpec(memory_space=pl.ANY)] * len(needs),
        out_specs=[by_rows, pl.BlockSpec((wide, ROWS), lambda i, order: (0, i))],
        scratch_shapes=[pltpu.VMEM((8, chan), jnp.float32)],
    )
    return pl.pallas_call(
        partial(conv_forward_kernel, min(256, chan)),
        grid_spec=spec,
        out_shape=[
            jax.ShapeDtypeStruct((length, chan), jnp.bfloat16),
            jax.ShapeDtypeStruct((wide, length), jnp.float32),
        ],
        compiler_params=pltpu.CompilerParams(vmem_limit_bytes=40 * 2**20),
        cost_estimate=pl.CostEstimate(
            flops=2 * wide * length * chan, bytes_accessed=22 * length * chan, transcendentals=length * chan
        ),
        name="conv_forward",
    )(order, x_part, conv_w, conv_b, sel_proj, *needs)


def conv_backward_kernel(
    lanes,
    order_ref, x_ref, before_ref, upart_ref, sgrad_ref, w_ref, b_ref, proj_ref, alog_ref,
    dec_ref, dbias_ref, dskip_ref, dproj_ref,
    *refs,
):
    xgrad_ref, stack_ref, head, wgrad, bgrad, pgrad = refs[-6:]
    rows, chan = x_ref.shape
    taps = w_ref.shape[0]
    last = pl.num_programs(0) - 1
    first = pl.program_id(0) == last

    @pl.when(pl.program_id(0) == 0)
    def _():
        head[...] = jnp.zeros_like(head)
        wgrad[...] = jnp.zeros_like(wgrad)
        bgrad[...] = jnp.zeros_like(bgrad)
        pgrad[...] = jnp.zeros_like(pgrad)

    sgrad = sgrad_ref[...].astype(jnp.bfloat16)
    for start in range(0, chan, lanes):
        at = pl.ds(start, lanes)
        earlier = before_ref[8:, at].astype(jnp.float32)
        window = jnp.concatenate([jnp.where(first, 0.0, earlier), x_ref[:, at].astype(jnp.float32)], axis=0)
        parts = taps_of(window, rows, taps)
        pre = b_ref[:, at] + sum(w_ref[tap : tap + 1, at] * part for tap, part in enumerate(parts))
        sig = 1.0 / (1.0 + jnp.exp(-pre))
        act = (pre * sig).astype(jnp.bfloat16)
        u_grad = upart_ref[:, at] + lax.dot_general(sgrad, proj_ref[:, at], TN, preferred_element_type=jnp.float32)
        grad = u_grad * (sig * (1.0 + pre * (1.0 - sig)))
        bgrad[:, at] += jnp.sum(grad, axis=0, keepdims=True)
        wgrad[:, at] += jnp.concatenate([jnp.sum(grad * part, axis=0, keepdims=True) for part in parts], axis=0)
        pgrad[:, at] += jnp.dot(sgrad, act, preferred_element_type=jnp.float32)
        later = jnp.concatenate([grad, head[:, at]], axis=0)
        head[:, at] = grad[:8, :]
        x_grad = sum(w_ref[tap : tap + 1, at] * later[taps - 1 - tap : taps - 1 - tap + rows, :] for tap in range(taps))
        xgrad_ref[:, at] = x_grad.astype(jnp.bfloat16)

    @pl.when(pl.program_id(0) == last)
    def _():
        half = chan // 2
        stack_ref[...] = jnp.zeros_like(stack_ref)
        terms = (pgrad[...], dproj_ref[...], dec_ref[...] * -jnp.exp(alog_ref[...]), wgrad[...], bgrad[...],
                 dbias_ref[...], dskip_ref[...])
        at = 0
        for term in terms:
            for side in range(2):
                stack_ref[side, at : at + term.shape[0], :] = term[:, side * half : (side + 1) * half]
            at += term.shape[0]


def conv_backward(order, x_part, u_part, select_grad, conv_w, conv_b, sel_proj, a_log, sums, needs=()):
    length, chan = x_part.shape
    wide = sel_proj.shape[0]
    count = length // ROWS
    high = -(-(wide + conv_w.shape[0] + 1 + sum(term.shape[0] for term in sums)) // 16) * 16
    whole = lambda shape: pl.BlockSpec(shape, lambda i, order: (0, 0))
    at = lambda i, order: order[count - 1 - i]
    by_rows = pl.BlockSpec((ROWS, chan), lambda i, order: (at(i, order), 0))
    before = pl.BlockSpec((16, chan), lambda i, order: ((order[lax.max(count - 2 - i, 0)] + 1) * (ROWS // 16) - 1, 0))
    spec = pltpu.PrefetchScalarGridSpec(
        num_scalar_prefetch=1,
        grid=(count,),
        in_specs=[
            by_rows,
            before,
            pl.BlockSpec((ROWS, chan), lambda i, order: (count - 1 - i, 0)),
            pl.BlockSpec((wide, ROWS), lambda i, order: (0, count - 1 - i)),
            whole(conv_w.shape),
            whole((1, chan)),
            whole((wide, chan)),
            whole(a_log.shape),
        ]
        + [whole(term.shape) for term in sums]
        + [pl.BlockSpec(memory_space=pl.ANY)] * len(needs),
        out_specs=[by_rows, pl.BlockSpec((2, high, chan // 2), lambda i, order: (0, 0, 0))],
        scratch_shapes=[
            pltpu.VMEM((8, chan), jnp.float32),
            pltpu.VMEM(conv_w.shape, jnp.float32),
            pltpu.VMEM((1, chan), jnp.float32),
            pltpu.VMEM((wide, chan), jnp.float32),
        ],
    )
    return pl.pallas_call(
        partial(conv_backward_kernel, min(256, chan)),
        grid_spec=spec,
        out_shape=[
            jax.ShapeDtypeStruct((length, chan), jnp.bfloat16),
            jax.ShapeDtypeStruct((2, high, chan // 2), jnp.float32),
        ],
        compiler_params=pltpu.CompilerParams(vmem_limit_bytes=40 * 2**20),
        cost_estimate=pl.CostEstimate(
            flops=4 * wide * length * chan, bytes_accessed=40 * length * chan, transcendentals=length * chan
        ),
        name="conv_backward",
    )(order, x_part, x_part, u_part, select_grad, conv_w, conv_b, sel_proj, a_log, *sums, *needs)


def weight_rows_kernel(x_ref, others_ref, in_ref, out_ref):
    group = others_ref.shape[0]
    cols = x_ref.shape[3] // 2
    inner = out_ref.shape[1]
    for place in range(group):
        for turn in range(2):
            at = (turn * group + place) * cols
            here = slice(turn * cols, (turn + 1) * cols)
            total = x_ref[0, place, :, here].astype(jnp.float32) + x_ref[1, place, :, here].astype(jnp.float32)
            in_ref[:, at : at + cols] = total
            in_ref[:, inner + at : inner + at + cols] = others_ref[place, :, here].astype(jnp.float32)
            out_cols = slice((2 + turn) * cols, (3 + turn) * cols)
            out_ref[:, at : at + cols] = others_ref[place, :, out_cols].astype(jnp.float32)


def weight_rows(x_pieces, others):
    group, rows, wide = others.shape
    inner = group * wide // 2
    return pl.pallas_call(
        weight_rows_kernel,
        out_shape=[
            jax.ShapeDtypeStruct((rows, 2 * inner), jnp.float32),
            jax.ShapeDtypeStruct((rows, inner), jnp.float32),
        ],
        compiler_params=pltpu.CompilerParams(vmem_limit_bytes=40 * 2**20),
        name="weight_rows",
    )(x_pieces, others)


def interleave_kernel(near_ref, far_ref, both_ref):
    both_ref[0, 0] = near_ref[0]
    both_ref[0, 1] = far_ref[0]


def interleave(near, far):
    group, rows, width = near.shape
    block = pl.BlockSpec((1, rows, width), lambda i: (i, 0, 0))
    both = pl.pallas_call(
        interleave_kernel,
        grid=(group,),
        in_specs=[block, block],
        out_specs=pl.BlockSpec((1, 2, rows, width), lambda i: (i, 0, 0, 0)),
        out_shape=jax.ShapeDtypeStruct((group, 2, rows, width), near.dtype),
        name="interleave",
    )(near, far)
    return both.reshape(-1, width)


def silu_slope(values):
    sigmoid_value = jax.nn.sigmoid(values)
    return sigmoid_value * (1.0 + values * (1.0 - sigmoid_value))


def tie(index, *needs):
    for need in needs:
        first = need.reshape(-1)[:1].reshape(())
        index = index + (first != first).astype(jnp.int32)
    return index


def swap(values, axis, bit=1):
    return lax.ppermute(values, axis, [(index, index ^ bit) for index in range(lax.axis_size(axis))])


def sum_over_group(values, axis, sent=jnp.float32):
    size = lax.axis_size("quarter")
    bits = [1 << place for place in range(size.bit_length() - 1)]
    count = max(len(bits), 1)
    done = []
    for turn, part in enumerate(jnp.split(values, count, axis=axis)):
        for bit in bits[turn:] + bits[:turn]:
            part = part + swap(part.astype(sent), "quarter", bit).astype(jnp.float32)
        done.append(part)
    return jnp.concatenate(done, axis=axis)


def spread(blocks):
    copies = jnp.broadcast_to(blocks[None], (lax.axis_size("quarter"),) + blocks.shape)
    return lax.all_to_all(copies, "quarter", split_axis=0, concat_axis=0, tiled=True)


def collect(terms):
    terms = terms.reshape(lax.axis_size("quarter"), -1, terms.shape[-1])
    return lax.all_to_all(terms, "quarter", split_axis=0, concat_axis=0, tiled=True)


def sum_over(values, axis):
    size = lax.axis_size(axis)
    for place in range(size.bit_length() - 1):
        values = values + swap(values, axis, 1 << place)
    return values


def own_columns(weight, start, cols, place):
    group = lax.axis_size("quarter")
    return jnp.concatenate(
        [lax.dynamic_slice_in_dim(weight, start + (place + turn * group) * cols, cols, 1) for turn in range(2)], axis=1
    )


def both_blocks(values, half):
    other = swap(values, "half")
    return jnp.concatenate([jnp.where(half == 0, values, other), jnp.where(half == 0, other, values)], axis=-1)


def reduce_rows_by_swaps(terms):
    size, index = lax.axis_size("fsdp"), lax.axis_index("fsdp")
    terms = terms.reshape(size, -1, terms.shape[-1])
    for place in range(size.bit_length() - 1):
        bit = lax.rem(index >> place, 2)
        pairs = terms.reshape((-1, 2) + terms.shape[1:])
        kept, sent = [lax.dynamic_index_in_dim(pairs, which, 1, keepdims=False) for which in (bit, 1 - bit)]
        got = swap(sent.astype(jnp.bfloat16), "fsdp", 1 << place)
        terms = kept.astype(jnp.float32) + got.astype(jnp.float32)
    return terms[0]


def reduce_rows(terms, axis):
    return lax.psum_scatter(terms, axis, scatter_dimension=0, tiled=True)


def in_order(half, mine, other):
    return jnp.stack([jnp.where(half == 0, mine, other), jnp.where(half == 0, other, mine)])


def shards(
    hidden_in,
    cotangent,
    lengths,
    norm_gain,
    w_in,
    conv_w,
    conv_b,
    x_proj,
    dt_proj_w,
    dt_bias,
    a_log,
    d_skip,
    w_out,
):
    half, place = lax.axis_index("half"), lax.axis_index("quarter")
    group = lax.axis_size("quarter")
    rows_dev, width = hidden_in.shape[1:]
    length = 2 * group * rows_dev
    mid = length // 2
    cols = conv_b.shape[0]
    inner = w_out.shape[1]
    states, low_rank = a_log.shape[0], dt_proj_w.shape[0]
    taps = conv_w.shape[0]
    bf16, f32 = jnp.bfloat16, jnp.float32
    pick = lambda values, which: lax.dynamic_index_in_dim(values, which, 0, keepdims=False)

    flat = hidden_in.astype(f32)
    inverse = lax.rsqrt(jnp.mean(flat * flat, axis=-1, keepdims=True) + EPS)
    scaled = flat * inverse
    normed = (scaled * norm_gain).astype(bf16)
    crossed = swap(pick(normed, 1 - half), "half")
    near = spread(pick(normed, half))
    far = spread(gate([crossed], near)[0])

    later = lax.optimization_barrier((place, normed))[0]
    w_x = lax.all_gather(own_columns(w_in, 0, cols, later), "fsdp", axis=0, tiled=True)
    w_z = lax.all_gather(own_columns(w_in, inner, cols, later), "fsdp", axis=0, tiled=True)
    w_o = lax.all_gather(own_columns(w_out, 0, cols, later), "fsdp", axis=0, tiled=True)

    x_near, x_far = [
        jnp.dot(rows.reshape(mid, width), w_x, preferred_element_type=f32).astype(bf16) for rows in (near, far)
    ]
    x_part = jnp.stack([part.reshape(group, rows_dev, -1) for part in (x_near, x_far)], axis=1).reshape(length, -1)
    tokens = interleave(near, far)
    cot_other = pick(cotangent, tie(1 - half, far))

    blocks = lax.iota(jnp.int32, 2 * group)
    order = lax.rem(blocks, group) * 2 + (blocks // group != half).astype(jnp.int32)
    time_block = (lax.rem(blocks, 2) ^ half) * group + blocks // 2
    position = (time_block[:, None] * rows_dev + lax.iota(jnp.int32, rows_dev)[None]).reshape(length, 1)

    small = jnp.concatenate([conv_w, conv_b[None], dt_bias[None], a_log, d_skip[None]], axis=0)
    small = both_blocks(lax.optimization_barrier((small, crossed))[0], half)
    conv_taps, conv_bias, step_bias = small[:taps], small[taps : taps + 1], small[taps + 1]
    log_rates, skip = small[taps + 2 : taps + 2 + states], small[taps + 2 + states]
    proj = both_blocks(lax.optimization_barrier((jnp.concatenate([x_proj, dt_proj_w], axis=0), crossed))[0], half)
    sel_proj, size_proj = proj[: x_proj.shape[0]], proj[x_proj.shape[0] :]

    u_act, select_part = conv_forward(order, x_part, conv_taps, conv_bias, sel_proj)
    select = sum_over_group(select_part, 1)

    cot_near = spread(pick(cotangent, tie(half, select)))
    cot_crossed = swap(gate([cot_other], select)[0], "half")
    blank = jnp.zeros((states, 2 * cols), f32)
    y_sent, held, delta, sig, _ = scan_forward(
        order, 0, 2 * group, select, u_act, size_proj, step_bias, log_rates, skip, blank
    )
    cot_far = spread(gate([cot_crossed], y_sent)[0])
    w_z = gate([w_z], y_sent)[0]
    z_part = jnp.dot(tokens, w_z, preferred_element_type=f32)
    z_gate = jax.nn.silu(z_part)
    valid = (position < pick(lengths, half)).astype(f32)
    y_float = y_sent.astype(f32)
    gated = lax.optimization_barrier((valid * y_float * z_gate).astype(bf16))
    branch_terms = lax.dot_general(gated, w_o, NT, preferred_element_type=f32).astype(bf16)
    branch_got = collect(branch_terms)

    cot = interleave(gate([cot_near], y_sent)[0], gate([cot_far], z_part, branch_terms)[0])
    gated_grad = valid * jnp.dot(cot, w_o, preferred_element_type=f32)
    y_grad = (gated_grad * z_gate).astype(bf16)
    z_grad = (gated_grad * y_float * silu_slope(z_part)).astype(bf16)
    y_grad, z_grad = lax.optimization_barrier((y_grad, z_grad))
    out_term = lax.dot_general(cot, gated, TN, preferred_element_type=f32).astype(bf16)
    out_rows = reduce_rows(out_term, "fsdp")
    z_term = lax.dot_general(tokens, z_grad, TN, preferred_element_type=f32).astype(bf16)
    z_rows = reduce_rows(z_term, "fsdp")

    sums = (blank, jnp.zeros((1, 2 * cols), f32), jnp.zeros((1, 2 * cols), f32), jnp.zeros((low_rank, 2 * cols), f32))
    u_part, select_part, *sums, _ = scan_backward(
        order, 0, 2 * group, select, held, blank, delta, sig, u_act, y_grad, size_proj, log_rates, skip, blank, sums,
        needs=[out_term, z_term, branch_terms],
    )
    select_part = gate([select_part], branch_got)[0]
    z_normed = lax.dot_general(z_grad, w_z, NT, preferred_element_type=f32).astype(bf16)
    select_grad = sum_over_group(select_part, 1, bf16)
    x_grad, stacked = conv_backward(
        order, x_part, u_part, select_grad, conv_taps, conv_bias, sel_proj, log_rates, sums, needs=[z_normed],
    )

    mine, other = pick(stacked, half), pick(stacked, 1 - half)
    other = swap(other.astype(bf16), "half")
    normed_terms = (lax.dot_general(x_grad, w_x, NT, preferred_element_type=f32) + z_normed).astype(bf16)
    normed_got = collect(gate([normed_terms], other)[0])
    x_term = lax.dot_general(tokens, gate([x_grad], normed_terms)[0], TN, preferred_element_type=f32).astype(bf16)
    x_term = lax.optimization_barrier(x_term)
    x_rows = reduce_rows_by_swaps(x_term).astype(bf16)
    others = reduce_rows(jnp.concatenate(gate([z_rows, out_rows], select_grad), axis=1), "half")
    others = others.reshape(group, -1, 4 * cols)

    stacked = sum_over(mine + other.astype(f32), "fsdp")

    normed_grad = jnp.sum(normed_got.reshape(group, 2, rows_dev, width).astype(f32), axis=0)
    far_normed = swap(normed_grad[1].astype(bf16), "half")
    branch = jnp.sum(branch_got.reshape(group, 2, rows_dev, width).astype(f32), axis=0)
    far_branch = swap(gate([branch[1].astype(bf16)], far_normed)[0], "half")
    normed_grad = in_order(half, normed_grad[0], far_normed.astype(f32))
    scaled_grad = normed_grad * norm_gain
    grad_in = cotangent.astype(f32) + inverse * (
        scaled_grad - scaled * jnp.mean(scaled_grad * scaled, axis=-1, keepdims=True)
    )

    branch = in_order(half, branch[0], far_branch.astype(f32))
    block_out = (flat + branch).astype(bf16)

    x_rows = x_rows.reshape(2 * group, -1, 2 * cols)
    x_rows = lax.all_to_all(x_rows, ("half", "quarter"), split_axis=0, concat_axis=0, tiled=True)
    others = lax.all_to_all(gate([others], x_rows, far_normed)[0], "quarter", split_axis=0, concat_axis=0, tiled=True)
    x_rows = x_rows.reshape((2, group) + x_rows.shape[1:])
    grad_w_in, grad_w_out = weight_rows(x_rows, others)

    gain_part = jnp.sum(w_x.astype(f32) * x_term + w_z.astype(f32) * z_term, axis=1)
    gain = gate([gain_part], far_normed)[0]
    for axis in ("quarter", "half", "fsdp"):
        gain = sum_over(gain, axis)

    pieces = []
    at = 0
    for count in (x_proj.shape[0], low_rank, states, taps, 1, 1, 1):
        pieces.append(stacked[at : at + count])
        at += count
    xproj, dtproj, alog, convw, convb, dtbias, dskip = pieces
    return (
        block_out,
        grad_in.astype(bf16),
        gain / norm_gain,
        grad_w_in,
        convw,
        convb[0],
        xproj,
        dtproj,
        dtbias[0],
        alog,
        dskip[0],
        grad_w_out,
    )


def solution(mesh):
    fsdp, seq = mesh.devices.shape
    fine = Mesh(mesh.devices.reshape(fsdp, 2, seq // 2), ("fsdp", "half", "quarter"))
    both = ("half", "quarter")
    return jax.shard_map(
        shards,
        mesh=fine,
        in_specs=(
            P("fsdp", both, None),
            P("fsdp", both, None),
            P("fsdp"),
            P(),
            P("fsdp", None),
            P(None, both),
            P(both),
            P(None, both),
            P(None, both),
            P(both),
            P(None, both),
            P(both),
            P("fsdp", None),
        ),
        out_specs=(
            P("fsdp", both, None),
            P("fsdp", both, None),
            P(),
            P(("fsdp",) + both, None),
            P(None, both),
            P(both),
            P(None, both),
            P(None, both),
            P(both),
            P(None, both),
            P(both),
            P(("fsdp",) + both, None),
        ),
        check_vma=False,
    )
```
